32 devices in a mesh: src: 4 (over y, x), tgt: 8 (over z, core).
Axes of the slice: x: 2, y: 2, z: 4, core: 2. Of those that a mesh axis runs over, the one named last changes fastest.
Arguments:
- incident: bfloat16 [4, 1024, 2048], P('src', 'tgt'), may hold values from -6 to 6
- factors: bfloat16 [12, 4, 1024, 32, 128], P(None, 'src', 'tgt'), may hold values from -0.5 to 0.5
- near_blocks: bfloat16 [4, 1024, 32, 512], P('src', 'tgt'), may hold values from -0.25 to 0.25
- near_lists: int32 [4, 1024, 8], P('src', 'tgt'), may hold values from 0 to 8
Outputs:
- scattered: float32 [4, 1024, 2048], P('src', 'tgt')
The draws below stay inside these ranges and needn't reach their ends.
Inputs may be any that keep to these rules, and one draw needn't show every extreme that they name: `near_lists`: offset o of block q names source block q + o - 4 of the same row; offsets may repeat within a list.
All inputs are finite; a program needn't handle non-finite values.
Results may differ from the reference program's by a relative error of at most 0.014.
Values may be sent and summed in bfloat16 or wider, within the bound.
No kernel may reach another device: no remote copies, remote signals or barrier semaphores. Data moves between devices by JAX's collectives and lax.ppermute only.
A program may use at most 128 MiB of HBM per device.

```python
import jax
import jax.numpy as jnp
from jax import lax

R = 32
F = 32
LB = 128
K = 8
HW = 4
SRC_BITS = 2
TGT_BITS = 3
LEVELS_A = 4
LEVELS_B = 3
LEVELS = 12
ROW = 1024
N_SRC = 4
N_TGT = 8


def with_ends(result, stream_key, least, top_value):
    longest = result.shape.index(max(result.shape))
    spots = []
    for shift in (0, 1):
        where = [jax.random.randint(jax.random.fold_in(stream_key, axis), (), 0, length) for axis, length in enumerate(result.shape)]
        where[longest] = (where[longest] + shift) % result.shape[longest]
        spots.append(tuple(where))
    return result.at[spots[0]].set(least).at[spots[1]].set(top_value)


def shard_levels(stream_key, dims, cuts, least, top_value):
    loudness = 1.0
    for dim, blocks in cuts:
        steps = jax.random.uniform(jax.random.fold_in(jax.random.fold_in(stream_key, 6), dim), (blocks,), jnp.float32, least / len(cuts), top_value / len(cuts))
        loudness = loudness * jnp.repeat(jnp.exp(steps), dims[dim] // blocks).reshape((-1,) + (1,) * (len(dims) - 1 - dim))
    return loudness


def normal_values(rng, extent, scale, limit, cuts=(), held_as=jnp.bfloat16):
    values = jax.random.normal(rng, extent, jnp.float32) * scale
    if len(cuts) > 0:
        values = shard_levels(rng, extent, cuts, -0.22, 0.18) * values
    return jnp.clip(values, min=-limit, max=limit).astype(held_as)


def setup_inputs(seed: int = 0) -> dict:
    key_list = jax.random.split(jax.random.key(seed), 5)
    return {
        "incident": normal_values(key_list[0], (N_SRC, ROW, R * 2 * F), 1.0, 6.0, ((0, 4), (1, 8))),
        "factors": normal_values(key_list[1], (LEVELS, N_SRC, ROW, R, 4 * R), (4 * R) ** -0.5, 0.5, ((1, 4), (2, 8))),
        "near_blocks": normal_values(key_list[2], (N_SRC, ROW, R, K * 2 * R), (2 * K * R) ** -0.5, 0.25, ((0, 4), (1, 8))),
        "near_lists": with_ends(jax.random.randint(key_list[3], (N_SRC, ROW, K), 0, 2 * HW + 1), jax.random.fold_in(key_list[3], 1), 0, 2 * HW).astype(jnp.int32),
    }


def combine(products, fields):
    real_part = products[0][..., :fields] - products[1][..., fields:]
    imag_part = products[0][..., fields:] + products[1][..., :fields]
    return jnp.concatenate([real_part, imag_part], axis=-1)


def mix_level(own_part, partner, weights):
    stacked = jnp.concatenate([own_part, partner], axis=1).astype(jnp.float32)
    nblock, rows = weights.shape[0], weights.shape[1]
    mats = weights.astype(jnp.float32).reshape(nblock, rows, 2, 2 * rows)
    products = jnp.einsum('bipc,bcf->pbif', mats, stacked)
    return combine(products, own_part.shape[2] // 2)


def partner_flip(vector, along, step_bit):
    dims_old = vector.shape
    size_bit = 2 ** step_bit
    dims_new = dims_old[:along] + (dims_old[along] // (2 * size_bit), 2, size_bit) + dims_old[along + 1:]
    return jnp.flip(vector.reshape(dims_new), axis=along + 1).reshape(dims_old)


def apply_level(vector, partner, weights, result_f32):
    row_width = vector.shape[-1]

    def one_row(pieces):
        return mix_level(pieces[0].reshape(-1, R, row_width), pieces[1].reshape(-1, R, row_width), pieces[2].reshape(-1, R, 4 * R))

    mixed = lax.map(one_row, (vector, partner, weights)).reshape(vector.shape)
    if result_f32:
        return mixed
    return mixed.astype(jnp.bfloat16)


def reference(incident, factors, near_blocks, near_lists):
    row_width = 2 * F
    vector = incident.reshape(N_SRC, N_TGT, LB, R, row_width)
    factor_all = factors.reshape(LEVELS, N_SRC, N_TGT, LB, R, 4 * R)
    level = 0
    for step_bit in range(SRC_BITS):
        vector = apply_level(vector, partner_flip(vector, 0, step_bit), factor_all[level], False)
        level += 1
    for step_bit in range(LEVELS_A):
        vector = apply_level(vector, partner_flip(vector, 2, step_bit), factor_all[level], False)
        level += 1
    vector = vector.reshape(N_SRC, N_TGT, N_TGT, LB // N_TGT, R, row_width)
    vector = jnp.swapaxes(vector, 1, 2).reshape(N_SRC, N_TGT, LB, R, row_width)
    for step_bit in range(LEVELS_B):
        vector = apply_level(vector, partner_flip(vector, 2, LEVELS_A + step_bit), factor_all[level], False)
        level += 1
    for step_bit in range(TGT_BITS):
        vector = apply_level(vector, partner_flip(vector, 1, step_bit), factor_all[level], level == LEVELS - 1)
        level += 1

    rows_all = incident.reshape(N_SRC, ROW, R, row_width)
    padded = jnp.pad(rows_all, ((0, 0), (HW, HW), (0, 0), (0, 0)))
    near_index = jnp.arange(ROW, dtype=jnp.int32)[None, :, None] + near_lists.astype(jnp.int32)

    def near_row(pieces):
        window, index_row, mats = pieces
        gathered = window[index_row].astype(jnp.float32)
        near_mats = mats.astype(jnp.float32).reshape(ROW, R, K, 2, R)
        products = jnp.einsum('bikpj,bkjf->pbif', near_mats, gathered)
        return combine(products, F)

    near_part = lax.map(near_row, (padded, near_index, near_blocks))
    total = near_part + vector.reshape(N_SRC, ROW, R, row_width)
    return total.reshape(N_SRC, ROW, R * row_width)
```

```python
import functools

import jax
import jax.numpy as jnp
from jax import lax
from jax.experimental import pallas as pl
from jax.experimental.pallas import tpu as pltpu
from jax.sharding import PartitionSpec as P

HW = 4
BF = jnp.bfloat16
F32 = jnp.float32
VMEM_LIMIT = 40 * 1024 * 1024


def lane_of(x):
    return lax.broadcasted_iota(jnp.int32, x.shape, 1)


def half_swap(x):
    return pltpu.roll(x, x.shape[1] // 2, 1)


def times_i(x):
    width = x.shape[1]
    quarter = width // 4
    low = pltpu.roll(x, quarter, 1)
    high = pltpu.roll(x, width - quarter, 1)
    return jnp.where(lane_of(x) % (2 * quarter) < quarter, -high, low)


def pick_diag(res):
    rows = res.shape[0] // 2
    top, bottom = res[:rows], res[rows:]
    return jnp.where(lane_of(top) < res.shape[1] // 2, top, bottom)


def with_turn(x):
    return x, times_i(x.astype(F32)).astype(BF)


def mix(own, own_i, other, other_i, weights):
    stacked = jnp.concatenate([own, other, own_i, other_i], axis=0)
    res = lax.dot_general(
        weights, stacked, (((1,), (0,)), ((), ())), preferred_element_type=F32
    )
    return pick_diag(res)


def take_weights(w_ref, group, m, lows):
    w = w_ref[0, pl.ds(group * lows + 2 * m, 2)]
    return w.reshape(2 * w.shape[1], w.shape[2])


def params():
    return pltpu.CompilerParams(vmem_limit_bytes=VMEM_LIMIT)


def cost(blocks):
    return pl.CostEstimate(
        flops=blocks * 2 * 64 * 128 * 64, bytes_accessed=blocks * 16384, transcendentals=0
    )


def full(shape):
    zeros = (0,) * len(shape)
    return pl.BlockSpec(shape, lambda i, t: zeros)


def chunk_weights(factors, level, r, groups_in, lows):
    _, _, rows, cols = factors.shape
    return pl.BlockSpec(
        (1, groups_in * lows, rows, cols), lambda i, t: (level, (t[0] // groups_in) ^ r, 0, 0)
    )


def call(kernel, tgt_index, arrays, in_specs, out_shapes, out_specs, scratch, blocks, aliases=None):
    return pl.pallas_call(
        kernel,
        out_shape=out_shapes,
        grid_spec=pltpu.PrefetchScalarGridSpec(
            num_scalar_prefetch=1,
            grid=(1,),
            in_specs=in_specs,
            out_specs=out_specs,
            scratch_shapes=scratch,
        ),
        compiler_params=params(),
        cost_estimate=cost(blocks),
        input_output_aliases=aliases or {},
    )(tgt_index, *arrays)


def convert_kernel(G, lows, t, inc_ref, out_ref, wide, tall):
    half = lows // 2
    rank = out_ref.shape[2]
    for j in range(rank // 2):
        wide[j] = inc_ref[:, pl.ds(j * 128, 128)].astype(F32)
    for b in range(G):
        group = (t[0] % G) ^ b
        for j in range(rank // 2):
            even = wide[j, pl.ds(group * lows, half, stride=2), :]
            odd = wide[j, pl.ds(group * lows + 1, half, stride=2), :]
            low = lane_of(even) < 64
            tall[pl.ds(b * half * rank + 2 * j, half, stride=rank), :] = jnp.where(
                low, even, half_swap(odd)
            )
            tall[pl.ds(b * half * rank + 2 * j + 1, half, stride=rank), :] = jnp.where(
                low, half_swap(even), odd
            )
    out_ref[...] = tall[...].astype(BF).reshape(out_ref.shape)


def level_kernel(G, lows, flip, t, own_ref, other_ref, w_ref, out_ref):
    half = lows // 2
    for b in range(G):
        group = (t[0] % G) ^ b
        for m in range(half):
            own, own_i = with_turn(own_ref[b, m])
            other, other_i = with_turn(other_ref[b ^ flip, m])
            out_ref[b, m] = mix(
                own, own_i, other, other_i, take_weights(w_ref, group, m, lows)
            ).astype(BF)


def split_kernel(G, lows, low_bits, t, own_ref, other_ref, *rest):
    w_refs = rest[: 1 + low_bits]
    out_refs = rest[1 + low_bits : 1 + low_bits + G]
    half = lows // 2
    for b in range(G):
        group = (t[0] % G) ^ b
        values = []
        for m in range(half):
            own, own_i = with_turn(own_ref[b, m])
            other, other_i = with_turn(other_ref[b, m])
            values.append(
                mix(own, own_i, other, other_i, take_weights(w_refs[0], group, m, lows))
            )
        for bit in range(low_bits):
            pairs = [(x.astype(BF), times_i(x).astype(BF)) for x in values]
            new = []
            for m in range(half):
                own, own_i = pairs[m]
                if bit == 0:
                    other32 = half_swap(own.astype(F32))
                    other, other_i = other32.astype(BF), times_i(other32).astype(BF)
                else:
                    other, other_i = pairs[m ^ (1 << (bit - 1))]
                new.append(
                    mix(own, own_i, other, other_i, take_weights(w_refs[1 + bit], group, m, lows))
                )
            values = new
        for m in range(half):
            out_refs[b][m] = values[m].astype(BF)


def group_kernel(G, lows, groups, t, *refs):
    bits = groups.bit_length() - 1
    ins = refs[:groups]
    w_refs = refs[groups : groups + bits]
    outs = refs[groups + bits : groups + bits + groups // G]
    half = lows // 2

    def one(m):
        values = None
        pairs = [with_turn(ins[g][m]) for g in range(groups)]
        for bit in range(bits):
            values = [
                mix(
                    *pairs[g],
                    *pairs[g ^ (1 << bit)],
                    take_weights(w_refs[bit], t[0] ^ g, m, lows),
                )
                for g in range(groups)
            ]
            if bit < bits - 1:
                pairs = [(x.astype(BF), times_i(x).astype(BF)) for x in values]
        for g in range(groups):
            outs[g // G][g % G, m] = values[g].astype(BF)

    def body(m, carry):
        one(m)
        return carry

    lax.fori_loop(0, half, body, 0)


def final_kernel(G, lows, flip, t, own_ref, other_ref, w_ref, near_ref, *rest):
    out_ref, tall, wide = rest[-3:]
    half = lows // 2
    rank = own_ref.shape[2]
    for b in range(G):
        group = (t[0] % G) ^ b
        for m in range(half):
            own, own_i = with_turn(own_ref[b, m])
            other, other_i = with_turn(other_ref[b ^ flip, m])
            tall[pl.ds((b * half + m) * rank, rank), :] = (
                mix(own, own_i, other, other_i, take_weights(w_ref, group, m, lows))
                + near_ref[group * half + m]
            )
    for b in range(G):
        group = (t[0] % G) ^ b
        for j in range(rank // 2):
            first = tall[pl.ds(b * half * rank + 2 * j, half, stride=rank), :]
            second = tall[pl.ds(b * half * rank + 2 * j + 1, half, stride=rank), :]
            low = lane_of(first) < 64
            wide[j, pl.ds(group * lows, half, stride=2), :] = jnp.where(
                low, first, half_swap(second)
            )
            wide[j, pl.ds(group * lows + 1, half, stride=2), :] = jnp.where(
                low, half_swap(first), second
            )
    for j in range(rank // 2):
        out_ref[:, pl.ds(j * 128, 128)] = wide[j]


def near_kernel(G, lows, chunks, count, near_count, t, lists, *refs):
    v_refs = refs[:chunks]
    below_ref, above_ref, mats_ref, out_ref, window = refs[chunks : chunks + 5]
    half = lows // 2
    rank = v_refs[0].shape[2]

    def put(place, x):
        wide = x.astype(F32)
        low = lane_of(wide) < 64
        swapped = half_swap(wide)
        for side, dup in enumerate((jnp.where(low, wide, swapped), jnp.where(low, swapped, wide))):
            window[place + side, 0:rank, :] = dup.astype(BF)
            window[place + side, rank : 2 * rank, :] = times_i(dup).astype(BF)

    @pl.when(pl.program_id(0) == 0)
    def _():
        for e in range(HW // 2):
            put(2 * e, below_ref[e])
            put(HW + G * chunks * lows + 2 * e, above_ref[e])
        for r in range(chunks):
            for b in range(G):
                group = t[0] ^ (r * G + b)
                for m in range(half):
                    put(HW + group * lows + 2 * m, v_refs[r][b, m])

    base = pl.program_id(0) * count
    last = None
    for n in range(count):
        parts = [window[base + n + lists[base + n, k]] for k in range(near_count)]
        stacked = jnp.concatenate(parts, axis=0)
        res = lax.dot_general(
            mats_ref[n], stacked, (((1,), (0,)), ((), ())), preferred_element_type=F32
        )
        if n % 2 == 0:
            last = res
        else:
            out_ref[n // 2] = jnp.where(lane_of(res) < 64, last, res)


def near_field(tgt_index, lists, mats, chunks, below, above, G, lows):
    blocks, rank, cols = mats.shape
    near_count = lists.shape[1]
    count = 16
    v_shape = chunks[0].shape

    def spec(shape):
        zeros = (0,) * len(shape)
        return pl.BlockSpec(shape, lambda i, t, o: zeros)

    return pl.pallas_call(
        functools.partial(near_kernel, G, lows, len(chunks), count, near_count),
        out_shape=jax.ShapeDtypeStruct((blocks // 2, rank, 128), F32),
        grid_spec=pltpu.PrefetchScalarGridSpec(
            num_scalar_prefetch=2,
            grid=(blocks // count,),
            in_specs=[spec(v_shape) for _ in chunks]
            + [spec(below.shape), spec(above.shape)]
            + [pl.BlockSpec((count, rank, cols), lambda i, t, o: (i, 0, 0))],
            out_specs=pl.BlockSpec((count // 2, rank, 128), lambda i, t, o: (i, 0, 0)),
            scratch_shapes=[pltpu.VMEM((blocks + 2 * HW, 2 * rank, 128), BF)],
        ),
        compiler_params=params(),
        cost_estimate=pl.CostEstimate(
            flops=2 * blocks * rank * cols * 128, bytes_accessed=mats.size * 2, transcendentals=0
        ),
    )(tgt_index, lists, *chunks, below, above, mats)


def swapped_with(x, axis, distance):
    count = lax.axis_size(axis)
    return lax.ppermute(x, axis, [(i, i ^ distance) for i in range(count)])


def per_device(incident, factors, near_blocks, near_lists):
    groups = lax.axis_size("tgt")
    src_bits = lax.axis_size("src").bit_length() - 1
    tgt_bits = groups.bit_length() - 1
    blocks = incident.shape[1]
    rank = near_blocks.shape[2]
    lows = blocks // groups
    half = lows // 2
    low_bits = lows.bit_length() - 1
    G = 2
    chunks = groups // G
    order = list(range(chunks))[::-1]
    tgt_index = lax.axis_index("tgt").astype(jnp.int32).reshape(1)
    weights = factors[:, 0]
    chunk_shape = (G, half, rank, 128)
    chunk_out = jax.ShapeDtypeStruct(chunk_shape, BF)
    group_out = jax.ShapeDtypeStruct(chunk_shape[1:], BF)

    def chunk_rows(r, width):
        return pl.BlockSpec((G * lows, width), lambda i, t: ((t[0] // G) ^ r, 0))

    def wspec(level, r):
        return chunk_weights(weights, level, r, G, lows)

    def level_call(level, r, own, other, flip=0):
        return call(
            functools.partial(level_kernel, G, lows, flip),
            tgt_index,
            (own, other, weights),
            [full(chunk_shape), full(chunk_shape), wspec(level, r)],
            chunk_out,
            full(chunk_shape),
            [],
            G * lows,
        )

    width = incident.shape[2]
    v = [None] * chunks
    for r in order:
        v[r] = call(
            functools.partial(convert_kernel, G, lows),
            tgt_index,
            (incident[0],),
            [chunk_rows(r, width)],
            chunk_out,
            full(chunk_shape),
            [
                pltpu.VMEM((rank // 2, G * lows, 128), F32),
                pltpu.VMEM((G * half * rank, 128), F32),
            ],
            G * lows,
        )
    start = list(v)

    level = 0
    for bit in range(src_bits - 1):
        for r in order:
            v[r] = level_call(level, r, v[r], swapped_with(v[r], "src", 1 << bit))
        level += 1
    arrived = [None] * groups
    for r in order:
        partner = swapped_with(v[r], "src", 1 << (src_bits - 1))
        parts = call(
            functools.partial(split_kernel, G, lows, low_bits),
            tgt_index,
            (v[r], partner) + (weights,) * (1 + low_bits),
            [full(chunk_shape), full(chunk_shape)]
            + [wspec(level + k, r) for k in range(1 + low_bits)],
            [group_out] * G,
            [full(chunk_shape[1:])] * G,
            [],
            (1 + low_bits) * G * lows,
        )
        for b in range(G):
            g = r * G + b
            arrived[g] = swapped_with(parts[b], "tgt", g) if g else parts[b]
    level += 1 + low_bits

    edge = HW // 2
    ups = [(i, i + 1) for i in range(groups - 1)]
    downs = [(i + 1, i) for i in range(groups - 1)]
    rows_in = incident[0]
    first, last = edge_pairs(rows_in, rank)
    below = lax.ppermute(last, "tgt", ups)
    above = lax.ppermute(first, "tgt", downs)
    near = near_field(tgt_index, near_lists[0], near_blocks[0], start, below, above, G, lows)

    v = call(
        functools.partial(group_kernel, G, lows, groups),
        tgt_index,
        tuple(arrived) + (weights,) * tgt_bits,
        [full(chunk_shape[1:])] * groups
        + [
            pl.BlockSpec((1, blocks, rank, 128), functools.partial(lambda l, i, t: (l, 0, 0, 0), level + k))
            for k in range(tgt_bits)
        ],
        [chunk_out] * chunks,
        [full(chunk_shape)] * chunks,
        [],
        tgt_bits * blocks,
    )
    v = list(v)
    level += tgt_bits
    for bit in range(tgt_bits - 1):
        distance = 1 << bit
        others = [swapped_with(v[r ^ (distance // G)], "tgt", distance) for r in range(chunks)]
        v = [level_call(level, r, v[r], others[r], distance % G) for r in range(chunks)]
        level += 1
    out = None
    distance = 1 << (tgt_bits - 1)
    others = [swapped_with(v[r ^ (distance // G)], "tgt", distance) for r in range(chunks)]
    for r in range(chunks):
        partner = others[r]
        arrays = (v[r], partner, weights, near)
        specs = [
            full(chunk_shape),
            full(chunk_shape),
            wspec(level, r),
            pl.BlockSpec(
                (G * half, rank, 128), functools.partial(lambda r, i, t: ((t[0] // G) ^ r, 0, 0), r)
            ),
        ]
        aliases = None
        if out is not None:
            arrays += (out,)
            specs += [pl.BlockSpec(memory_space=pl.ANY)]
            aliases = {5: 0}
        out = call(
            functools.partial(final_kernel, G, lows, distance % G),
            tgt_index,
            arrays,
            specs,
            jax.ShapeDtypeStruct((blocks, width), F32),
            chunk_rows(r, width),
            [
                pltpu.VMEM((G * half * rank, 128), F32),
                pltpu.VMEM((rank // 2, G * lows, 128), F32),
            ],
            G * lows,
            aliases,
        )
    return out[None]


def edge_pairs(rows_in, rank):
    def pairs(x):
        x = x.reshape(HW // 2, 2, rank, -1)
        return jnp.swapaxes(x, 1, 2).reshape(HW // 2, rank, -1)

    return pairs(rows_in[:HW]), pairs(rows_in[-HW:])


def solution(mesh):
    return jax.shard_map(
        per_device,
        mesh=mesh,
        in_specs=(
            P("src", "tgt", None),
            P(None, "src", "tgt", None, None),
            P("src", "tgt", None, None),
            P("src", "tgt", None),
        ),
        out_specs=P("src", "tgt", None),
        check_vma=False,
    )
```

```python
import functools

import jax
import jax.numpy as jnp
from jax import lax
from jax.experimental import pallas as pl
from jax.experimental.pallas import tpu as pltpu
from jax.sharding import PartitionSpec as P

HW = 4
BF = jnp.bfloat16
F32 = jnp.float32
CONV_US = 2.5
VMEM_LIMIT = 16 * 1024 * 1024


def lane_of(x):
    return lax.broadcasted_iota(jnp.int32, x.shape, 1)


def half_swap(x):
    return pltpu.roll(x, x.shape[1] // 2, 1)


def times_i(x):
    width = x.shape[1]
    quarter = width // 4
    low = pltpu.roll(x, quarter, 1)
    high = pltpu.roll(x, width - quarter, 1)
    return jnp.where(lane_of(x) % (2 * quarter) < quarter, -high, low)


def pick_diag(res):
    rows = res.shape[0] // 2
    top, bottom = res[:rows], res[rows:]
    return jnp.where(lane_of(top) < res.shape[1] // 2, top, bottom)


def with_turn(x):
    return x, times_i(x)


def mix(own, own_i, other, other_i, weights):
    stacked = jnp.concatenate([own, other, own_i, other_i], axis=0)
    res = lax.dot_general(
        weights, stacked, (((1,), (0,)), ((), ())), preferred_element_type=F32
    )
    return pick_diag(res)


def take_weights(w_ref, group, m, lows):
    w = w_ref[pl.ds(group * lows + 2 * m, 2)]
    return w.reshape(2 * w.shape[1], w.shape[2])


def params():
    return pltpu.CompilerParams(vmem_limit_bytes=VMEM_LIMIT)


def cost(us):
    return pl.CostEstimate(flops=0, bytes_accessed=int(us * 3.6e6), transcendentals=0)


def full(shape):
    zeros = (0,) * len(shape)
    return pl.BlockSpec(shape, lambda i, t: zeros)


def chunk_weights(weights, level, r, groups_in, lows):
    _, _, rows, cols = weights.shape
    return pl.BlockSpec(
        (None, groups_in * lows, rows, cols), lambda i, t: (level, (t[0] // groups_in) ^ r, 0, 0)
    )


def call(kernel, tgt_index, arrays, in_specs, out_shapes, out_specs, scratch, us, aliases=None):
    return pl.pallas_call(
        kernel,
        out_shape=out_shapes,
        grid_spec=pltpu.PrefetchScalarGridSpec(
            num_scalar_prefetch=1,
            grid=(1,),
            in_specs=in_specs,
            out_specs=out_specs,
            scratch_shapes=scratch,
        ),
        compiler_params=params(),
        cost_estimate=cost(us),
        input_output_aliases=aliases or {},
    )(tgt_index, *arrays)


def convert_kernel(G, lows, t, inc_ref, out_ref, wide, tall):
    half = lows // 2
    rank = out_ref.shape[2]
    for j in range(rank // 2):
        wide[j] = inc_ref[:, pl.ds(j * 128, 128)].astype(F32)
    for b in range(G):
        group = (t[0] % G) ^ b
        for j in range(rank // 2):
            even = wide[j, pl.ds(group * lows, half, stride=2), :]
            odd = wide[j, pl.ds(group * lows + 1, half, stride=2), :]
            low = lane_of(even) < 64
            tall[pl.ds(b * half * rank + 2 * j, half, stride=rank), :] = jnp.where(
                low, even, half_swap(odd)
            )
            tall[pl.ds(b * half * rank + 2 * j + 1, half, stride=rank), :] = jnp.where(
                low, half_swap(even), odd
            )
    out_ref[...] = tall[...].astype(BF).reshape(out_ref.shape)


def edge_kernel(rows, first_ref, last_ref, first_out, last_out, wide, tall):
    pairs, rank, _ = first_out.shape
    for ref, out, start in ((first_ref, first_out, 0), (last_ref, last_out, rows - HW)):
        for j in range(rank // 2):
            wide[j] = ref[:, pl.ds(j * 128, 128)].astype(F32)
        for j in range(rank // 2):
            even = wide[j, pl.ds(start, pairs, stride=2), :]
            odd = wide[j, pl.ds(start + 1, pairs, stride=2), :]
            low = lane_of(even) < 64
            tall[pl.ds(2 * j, pairs, stride=rank), :] = jnp.where(low, even, half_swap(odd))
            tall[pl.ds(2 * j + 1, pairs, stride=rank), :] = jnp.where(low, half_swap(even), odd)
        out[...] = tall[...].astype(BF).reshape(out.shape)


def edge_pairs(incident, rank):
    blocks, width = incident.shape
    rows, pairs = 16, HW // 2
    shape = jax.ShapeDtypeStruct((pairs, rank, 128), BF)
    return pl.pallas_call(
        functools.partial(edge_kernel, rows),
        grid=(1,),
        in_specs=[
            pl.BlockSpec((rows, width), lambda i: (0, 0)),
            pl.BlockSpec((rows, width), lambda i: (blocks // rows - 1, 0)),
        ],
        out_specs=[pl.BlockSpec(shape.shape, lambda i: (0, 0, 0))] * 2,
        out_shape=[shape] * 2,
        scratch_shapes=[pltpu.VMEM((rank // 2, rows, 128), F32), pltpu.VMEM((pairs * rank, 128), F32)],
        compiler_params=params(),
    )(incident, incident)


def level_kernel(G, lows, flip, t, own_ref, other_ref, w_ref, out_ref):
    half = lows // 2
    for b in range(G):
        group = (t[0] % G) ^ b
        for m in range(half):
            own, own_i = with_turn(own_ref[b, m])
            other, other_i = with_turn(other_ref[b ^ flip, m])
            out_ref[b, m] = mix(
                own, own_i, other, other_i, take_weights(w_ref, group, m, lows)
            ).astype(BF)


def split_kernel(G, lows, low_bits, t, own_ref, other_ref, *rest):
    w_refs = rest[: 1 + low_bits]
    out_refs = rest[1 + low_bits : 1 + low_bits + G]
    half = lows // 2
    keys = [(b, m) for b in range(G) for m in range(half)]
    groups = [(t[0] % G) ^ b for b in range(G)]
    pairs = {key: with_turn(own_ref[key]) for key in keys}
    others = {key: with_turn(other_ref[key]) for key in keys}
    for bit in range(-1, low_bits):
        if bit == 0:
            others = {key: with_turn(half_swap(pairs[key][0])) for key in keys}
        elif bit > 0:
            others = {(b, m): pairs[b, m ^ (1 << (bit - 1))] for b, m in keys}
        values = {
            (b, m): mix(
                *pairs[b, m],
                *others[b, m],
                take_weights(w_refs[1 + bit], groups[b], m, lows),
            ).astype(BF)
            for b, m in keys
        }
        pairs = {key: with_turn(x) for key, x in values.items()} if bit < low_bits - 1 else values
    for b, m in keys:
        out_refs[b][m] = pairs[b, m]


def group_kernel(G, lows, groups, t, *refs):
    bits = groups.bit_length() - 1
    ins = refs[:groups]
    w_refs = refs[groups : groups + bits]
    outs = refs[groups + bits : groups + bits + groups // G]
    half = lows // 2

    width = max(1, min(half, 32 // groups))
    keys = [(k, g) for k in range(width) for g in range(groups)]

    def body(step, carry):
        values = None
        pairs = {(k, g): with_turn(ins[g][step * width + k]) for k, g in keys}
        for bit in range(bits):
            values = {
                (k, g): mix(
                    *pairs[k, g],
                    *pairs[k, g ^ (1 << bit)],
                    take_weights(w_refs[bit], t[0] ^ g, step * width + k, lows),
                )
                for k, g in keys
            }
            if bit < bits - 1:
                pairs = {key: with_turn(x.astype(BF)) for key, x in values.items()}
        for k, g in keys:
            outs[g // G][g % G, step * width + k] = values[k, g].astype(BF)
        return carry

    lax.fori_loop(0, half // width, body, 0)


def final_kernel(G, lows, flip, t, own_ref, other_ref, w_ref, near_ref, *rest):
    out_ref, tall, wide = rest[-3:]
    half = lows // 2
    rank = own_ref.shape[2]
    for b in range(G):
        group = (t[0] % G) ^ b
        for m in range(half):
            own, own_i = with_turn(own_ref[b, m])
            other, other_i = with_turn(other_ref[b ^ flip, m])
            tall[pl.ds((b * half + m) * rank, rank), :] = (
                mix(own, own_i, other, other_i, take_weights(w_ref, group, m, lows))
                + near_ref[group * half + m]
            )
    for b in range(G):
        group = (t[0] % G) ^ b
        for j in range(rank // 2):
            first = tall[pl.ds(b * half * rank + 2 * j, half, stride=rank), :]
            second = tall[pl.ds(b * half * rank + 2 * j + 1, half, stride=rank), :]
            low = lane_of(first) < 64
            wide[j, pl.ds(group * lows, half, stride=2), :] = jnp.where(
                low, first, half_swap(second)
            )
            wide[j, pl.ds(group * lows + 1, half, stride=2), :] = jnp.where(
                low, half_swap(first), second
            )
    for j in range(rank // 2):
        out_ref[:, pl.ds(j * 128, 128)] = wide[j]


def near_kernel(G, lows, chunks, count, near_count, t, lists, *refs):
    v_refs = refs[:chunks]
    below_ref, above_ref, mats_ref, out_ref, window = refs[chunks : chunks + 5]
    half = lows // 2
    rank = v_refs[0].shape[2]

    row = lax.broadcasted_iota(jnp.int32, (128, 512), 0)
    col = lax.broadcasted_iota(jnp.int32, (128, 512), 1)
    turned = (col // 128) % 2 == 1
    low = col % 64 < 32
    lane = col % 64 + jnp.where(turned, jnp.where(low, 32, -32), 0)
    sign = jnp.where(turned & low, -1.0, 1.0)
    spread = jnp.where(row == col // 256 * 64 + lane, sign, 0.0).astype(BF)

    def put(places, x):
        wide = lax.dot_general(
            x.reshape(len(places) * rank, 128),
            spread,
            (((1,), (0,)), ((), ())),
            preferred_element_type=F32,
        ).astype(BF)
        for e, place in enumerate(places):
            for side in range(2):
                for turn in range(2):
                    first = 256 * side + 128 * turn
                    window[place + side, rank * turn : rank * (turn + 1), :] = wide[
                        e * rank : (e + 1) * rank, first : first + 128
                    ]

    @pl.when(pl.program_id(0) == 0)
    def _():
        put([2 * e for e in range(HW // 2)], below_ref[...])
        after = HW + G * chunks * lows
        put([after + 2 * e for e in range(HW // 2)], above_ref[...])
        for r in range(chunks):
            for b in range(G):
                group = t[0] ^ (r * G + b)
                put([HW + group * lows + 2 * m for m in range(half)], v_refs[r][b])

    base = pl.program_id(0) * count
    last = None
    for n in range(count):
        parts = [window[base + n + lists[base + n, k]] for k in range(near_count)]
        stacked = jnp.concatenate(parts, axis=0)
        res = lax.dot_general(
            mats_ref[n], stacked, (((1,), (0,)), ((), ())), preferred_element_type=F32
        )
        if n % 2 == 0:
            last = res
        else:
            out_ref[n // 2] = jnp.where(lane_of(res) < 64, last, res)


def near_field(tgt_index, lists, mats, chunks, below, above, G, lows):
    blocks, rank, cols = mats.shape
    near_count = lists.shape[1]
    count = 32
    v_shape = chunks[0].shape

    def spec(shape):
        zeros = (0,) * len(shape)
        return pl.BlockSpec(shape, lambda i, t, o: zeros)

    return pl.pallas_call(
        functools.partial(near_kernel, G, lows, len(chunks), count, near_count),
        out_shape=jax.ShapeDtypeStruct((blocks // 2, rank, 128), F32),
        grid_spec=pltpu.PrefetchScalarGridSpec(
            num_scalar_prefetch=2,
            grid=(blocks // count,),
            in_specs=[spec(v_shape) for _ in chunks]
            + [spec(below.shape), spec(above.shape)]
            + [pl.BlockSpec((count, rank, cols), lambda i, t, o: (i, 0, 0))],
            out_specs=pl.BlockSpec((count // 2, rank, 128), lambda i, t, o: (i, 0, 0)),
            scratch_shapes=[pltpu.VMEM((blocks + 2 * HW, 2 * rank, 128), BF)],
        ),
        compiler_params=params(),
        cost_estimate=cost(6.0),
    )(tgt_index, lists, *chunks, below, above, mats)


def swapped_with(x, axis, distance):
    count = lax.axis_size(axis)
    return lax.ppermute(x, axis, [(i, i ^ distance) for i in range(count)])


def per_device(incident, factors, near_blocks, near_lists):
    groups = lax.axis_size("tgt")
    src_bits = lax.axis_size("src").bit_length() - 1
    tgt_bits = groups.bit_length() - 1
    blocks = incident.shape[1]
    rank = near_blocks.shape[2]
    lows = blocks // groups
    half = lows // 2
    low_bits = lows.bit_length() - 1
    G = 2
    chunks = groups // G
    order = list(range(chunks))[::-1]
    tgt_index = lax.axis_index("tgt").astype(jnp.int32).reshape(1)
    weights = factors[:, 0]
    ends = {0: factors[:1, 0], factors.shape[0] - 1: factors[-1:, 0]}

    def level_weights(level):
        return (ends[level], 0) if level in ends else (weights, level)

    chunk_shape = (G, half, rank, 128)
    chunk_out = jax.ShapeDtypeStruct(chunk_shape, BF)
    group_out = jax.ShapeDtypeStruct(chunk_shape[1:], BF)

    def chunk_rows(r, width):
        return pl.BlockSpec((G * lows, width), lambda i, t: ((t[0] // G) ^ r, 0))

    def wspec(level, r):
        return chunk_weights(weights, level, r, G, lows)

    def level_call(level, r, own, other, flip=0):
        array, level = level_weights(level)
        return call(
            functools.partial(level_kernel, G, lows, flip),
            tgt_index,
            (own, other, array),
            [full(chunk_shape), full(chunk_shape), wspec(level, r)],
            chunk_out,
            full(chunk_shape),
            [],
            0.4,
        )

    ups = [(i, i + 1) for i in range(groups - 1)]
    downs = [(i + 1, i) for i in range(groups - 1)]
    first, last = edge_pairs(incident[0], rank)
    below = lax.ppermute(last, "tgt", ups)
    above = lax.ppermute(first, "tgt", downs)
    width = incident.shape[2]
    v = [None] * chunks
    for r in order:
        v[r] = call(
            functools.partial(convert_kernel, G, lows),
            tgt_index,
            (incident[0],),
            [chunk_rows(r, width)],
            chunk_out,
            full(chunk_shape),
            [
                pltpu.VMEM((rank // 2, G * lows, 128), F32),
                pltpu.VMEM((G * half * rank, 128), F32),
            ],
            CONV_US,
        )
    start = list(v)

    level = 0
    for bit in range(src_bits - 1):
        others = [swapped_with(v[r], "src", 1 << bit) for r in order]
        if bit == 0:
            others[-1], below, above = lax.optimization_barrier((others[-1], below, above))
        for r, other in zip(order, others):
            v[r] = level_call(level, r, v[r], other)
        level += 1
    arrived = [None] * groups
    for r in order:
        partner = swapped_with(v[r], "src", 1 << (src_bits - 1))
        parts = call(
            functools.partial(split_kernel, G, lows, low_bits),
            tgt_index,
            (v[r], partner) + (weights,) * (1 + low_bits),
            [full(chunk_shape), full(chunk_shape)]
            + [wspec(level + k, r) for k in range(1 + low_bits)],
            [group_out] * G,
            [full(chunk_shape[1:])] * G,
            [],
            1.5,
        )
        for b in range(G):
            g = r * G + b
            arrived[g] = swapped_with(parts[b], "tgt", g) if g else parts[b]
    level += 1 + low_bits

    near = near_field(tgt_index, near_lists[0], near_blocks[0], start, below, above, G, lows)

    v = call(
        functools.partial(group_kernel, G, lows, groups),
        tgt_index,
        tuple(arrived) + (weights,) * tgt_bits,
        [full(chunk_shape[1:])] * groups
        + [
            pl.BlockSpec(
                (None, blocks, rank, 128), functools.partial(lambda l, i, t: (l, 0, 0, 0), level + k)
            )
            for k in range(tgt_bits)
        ],
        [chunk_out] * chunks,
        [full(chunk_shape)] * chunks,
        [],
        2.5,
    )
    v = list(v)
    level += tgt_bits
    for bit in range(tgt_bits - 1):
        distance = 1 << bit
        others = [swapped_with(v[r ^ (distance // G)], "tgt", distance) for r in range(chunks)]
        v = [level_call(level, r, v[r], others[r], distance % G) for r in range(chunks)]
        level += 1
    out = None
    distance = 1 << (tgt_bits - 1)
    others = [swapped_with(v[r ^ (distance // G)], "tgt", distance) for r in range(chunks)]
    for r in range(chunks):
        partner = others[r]
        arrays = (v[r], partner, level_weights(level)[0], near)
        specs = [
            full(chunk_shape),
            full(chunk_shape),
            wspec(level_weights(level)[1], r),
            pl.BlockSpec(
                (G * half, rank, 128), functools.partial(lambda r, i, t: ((t[0] // G) ^ r, 0, 0), r)
            ),
        ]
        aliases = None
        if out is not None:
            arrays += (out,)
            specs += [pl.BlockSpec(memory_space=pl.ANY)]
            aliases = {5: 0}
        out = call(
            functools.partial(final_kernel, G, lows, distance % G),
            tgt_index,
            arrays,
            specs,
            jax.ShapeDtypeStruct((blocks, width), F32),
            chunk_rows(r, width),
            [
                pltpu.VMEM((G * half * rank, 128), F32),
                pltpu.VMEM((rank // 2, G * lows, 128), F32),
            ],
            1.2,
            aliases,
        )
    return out[None]


def solution(mesh):
    return jax.shard_map(
        per_device,
        mesh=mesh,
        in_specs=(
            P("src", "tgt", None),
            P(None, "src", "tgt", None, None),
            P("src", "tgt", None, None),
            P("src", "tgt", None),
        ),
        out_specs=P("src", "tgt", None),
        check_vma=False,
    )
```

```python
import functools

import jax
import jax.numpy as jnp
from jax import lax
from jax.experimental import pallas as pl
from jax.experimental.pallas import tpu as pltpu
from jax.sharding import PartitionSpec as P

HW = 4
BF = jnp.bfloat16
F32 = jnp.float32
CONV_US = 2.5
VMEM_LIMIT = 16 * 1024 * 1024


def lane_of(x):
    return lax.broadcasted_iota(jnp.int32, x.shape, 1)


def half_swap(x):
    return pltpu.roll(x, x.shape[1] // 2, 1)


def times_i(x):
    width = x.shape[1]
    quarter = width // 4
    low = pltpu.roll(x, quarter, 1)
    high = pltpu.roll(x, width - quarter, 1)
    return jnp.where(lane_of(x) % (2 * quarter) < quarter, -high, low)


def pick_diag(res):
    rows = res.shape[0] // 2
    top, bottom = res[:rows], res[rows:]
    return jnp.where(lane_of(top) < res.shape[1] // 2, top, bottom)


def with_turn(x):
    return x, times_i(x)


def mix(own, own_i, other, other_i, weights):
    stacked = jnp.concatenate([own, other, own_i, other_i], axis=0)
    res = lax.dot_general(
        weights, stacked, (((1,), (0,)), ((), ())), preferred_element_type=F32
    )
    return pick_diag(res)


def take_weights(w_ref, group, m, lows):
    w = w_ref[pl.ds(group * lows + 2 * m, 2)]
    return w.reshape(2 * w.shape[1], w.shape[2])


def params():
    return pltpu.CompilerParams(vmem_limit_bytes=VMEM_LIMIT)


def cost(us):
    return pl.CostEstimate(flops=0, bytes_accessed=int(us * 3.6e6), transcendentals=0)


def full(shape):
    zeros = (0,) * len(shape)
    return pl.BlockSpec(shape, lambda i, t: zeros)


def chunk_weights(weights, level, r, groups_in, lows):
    _, _, rows, cols = weights.shape
    return pl.BlockSpec(
        (None, groups_in * lows, rows, cols), lambda i, t: (level, (t[0] // groups_in) ^ r, 0, 0)
    )


def call(kernel, tgt_index, arrays, in_specs, out_shapes, out_specs, scratch, us, aliases=None):
    return pl.pallas_call(
        kernel,
        out_shape=out_shapes,
        grid_spec=pltpu.PrefetchScalarGridSpec(
            num_scalar_prefetch=1,
            grid=(1,),
            in_specs=in_specs,
            out_specs=out_specs,
            scratch_shapes=scratch,
        ),
        compiler_params=params(),
        cost_estimate=cost(us),
        input_output_aliases=aliases or {},
    )(tgt_index, *arrays)


def convert_kernel(G, lows, t, inc_ref, out_ref, wide, tall):
    half = lows // 2
    rank = out_ref.shape[2]
    for j in range(rank // 2):
        wide[j] = inc_ref[:, pl.ds(j * 128, 128)].astype(F32)
    for b in range(G):
        group = (t[0] % G) ^ b
        for j in range(rank // 2):
            even = wide[j, pl.ds(group * lows, half, stride=2), :]
            odd = wide[j, pl.ds(group * lows + 1, half, stride=2), :]
            low = lane_of(even) < 64
            tall[pl.ds(b * half * rank + 2 * j, half, stride=rank), :] = jnp.where(
                low, even, half_swap(odd)
            )
            tall[pl.ds(b * half * rank + 2 * j + 1, half, stride=rank), :] = jnp.where(
                low, half_swap(even), odd
            )
    out_ref[...] = tall[...].astype(BF).reshape(out_ref.shape)


def edge_kernel(rows, t, one_ref, two_ref, one_out, two_out, wide, tall):
    pairs, rank, _ = one_out.shape
    even_start = rows - HW
    odd = t[0] % 2
    starts = (even_start * (1 - odd), even_start * odd)
    for ref, out, start in zip((one_ref, two_ref), (one_out, two_out), starts):
        for j in range(rank // 2):
            wide[j] = ref[:, pl.ds(j * 128, 128)].astype(F32)
        for j in range(rank // 2):
            first = wide[j, pl.ds(start, pairs, stride=2), :]
            second = wide[j, pl.ds(start + 1, pairs, stride=2), :]
            low = lane_of(first) < 64
            tall[pl.ds(2 * j, pairs, stride=rank), :] = jnp.where(low, first, half_swap(second))
            tall[pl.ds(2 * j + 1, pairs, stride=rank), :] = jnp.where(
                low, half_swap(first), second
            )
        out[...] = tall[...].astype(BF).reshape(out.shape)


def edge_pairs(tgt_index, incident, rank):
    blocks, width = incident.shape
    rows, pairs = 16, HW // 2
    end = blocks // rows - 1
    shape = jax.ShapeDtypeStruct((pairs, rank, 128), BF)
    return pl.pallas_call(
        functools.partial(edge_kernel, rows),
        out_shape=[shape] * 2,
        grid_spec=pltpu.PrefetchScalarGridSpec(
            num_scalar_prefetch=1,
            grid=(1,),
            in_specs=[
                pl.BlockSpec((rows, width), lambda i, t: (end * (1 - t[0] % 2), 0)),
                pl.BlockSpec((rows, width), lambda i, t: (end * (t[0] % 2), 0)),
            ],
            out_specs=[full(shape.shape)] * 2,
            scratch_shapes=[
                pltpu.VMEM((rank // 2, rows, 128), F32),
                pltpu.VMEM((pairs * rank, 128), F32),
            ],
        ),
        compiler_params=params(),
    )(tgt_index, incident, incident)


def level_kernel(G, lows, flip, t, own_ref, other_ref, w_ref, out_ref):
    half = lows // 2
    for b in range(G):
        group = (t[0] % G) ^ b
        for m in range(half):
            own, own_i = with_turn(own_ref[b, m])
            other, other_i = with_turn(other_ref[b ^ flip, m])
            out_ref[b, m] = mix(
                own, own_i, other, other_i, take_weights(w_ref, group, m, lows)
            ).astype(BF)


def split_kernel(G, lows, low_bits, t, own_ref, other_ref, *rest):
    w_refs = rest[: 1 + low_bits]
    out_ref = rest[1 + low_bits]
    half = lows // 2
    keys = [(b, m) for b in range(G) for m in range(half)]
    groups = [(t[0] % G) ^ b for b in range(G)]
    pairs = {key: with_turn(own_ref[key]) for key in keys}
    others = {key: with_turn(other_ref[key]) for key in keys}
    for bit in range(-1, low_bits):
        if bit == 0:
            others = {key: with_turn(half_swap(pairs[key][0])) for key in keys}
        elif bit > 0:
            others = {(b, m): pairs[b, m ^ (1 << (bit - 1))] for b, m in keys}
        values = {
            (b, m): mix(
                *pairs[b, m],
                *others[b, m],
                take_weights(w_refs[1 + bit], groups[b], m, lows),
            ).astype(BF)
            for b, m in keys
        }
        pairs = {key: with_turn(x) for key, x in values.items()} if bit < low_bits - 1 else values
    for b, m in keys:
        out_ref[b, m] = pairs[b, m]


def group_kernel(G, lows, groups, t, *refs):
    bits = groups.bit_length() - 1
    ins = refs[:groups]
    w_refs = refs[groups : groups + bits]
    outs = refs[groups + bits : groups + bits + groups // G]
    half = lows // 2

    width = max(1, min(half, 32 // groups))
    keys = [(k, g) for k in range(width) for g in range(groups)]

    def body(step, carry):
        values = None
        pairs = {(k, g): with_turn(ins[g][step * width + k]) for k, g in keys}
        for bit in range(bits):
            values = {
                (k, g): mix(
                    *pairs[k, g],
                    *pairs[k, g ^ (1 << bit)],
                    take_weights(w_refs[bit], t[0] ^ g, step * width + k, lows),
                )
                for k, g in keys
            }
            if bit < bits - 1:
                pairs = {key: with_turn(x.astype(BF)) for key, x in values.items()}
        for k, g in keys:
            outs[g // G][g % G, step * width + k] = values[k, g].astype(BF)
        return carry

    lax.fori_loop(0, half // width, body, 0)


def final_kernel(G, lows, flip, t, own_ref, other_ref, w_ref, near_ref, *rest):
    out_ref, tall, wide = rest[-3:]
    half = lows // 2
    rank = own_ref.shape[2]
    for b in range(G):
        group = (t[0] % G) ^ b
        for m in range(half):
            own, own_i = with_turn(own_ref[b, m])
            other, other_i = with_turn(other_ref[b ^ flip, m])
            tall[pl.ds((b * half + m) * rank, rank), :] = (
                mix(own, own_i, other, other_i, take_weights(w_ref, group, m, lows))
                + near_ref[group * half + m]
            )
    for b in range(G):
        group = (t[0] % G) ^ b
        for j in range(rank // 2):
            first = tall[pl.ds(b * half * rank + 2 * j, half, stride=rank), :]
            second = tall[pl.ds(b * half * rank + 2 * j + 1, half, stride=rank), :]
            low = lane_of(first) < 64
            wide[j, pl.ds(group * lows, half, stride=2), :] = jnp.where(
                low, first, half_swap(second)
            )
            wide[j, pl.ds(group * lows + 1, half, stride=2), :] = jnp.where(
                low, half_swap(first), second
            )
    for j in range(rank // 2):
        out_ref[:, pl.ds(j * 128, 128)] = wide[j]


def near_kernel(G, lows, chunks, count, near_count, t, lists, *refs):
    v_refs = refs[:chunks]
    one_ref, two_ref, mats_ref, out_ref, window = refs[chunks : chunks + 5]
    half = lows // 2
    rank = v_refs[0].shape[2]

    row = lax.broadcasted_iota(jnp.int32, (128, 512), 0)
    col = lax.broadcasted_iota(jnp.int32, (128, 512), 1)
    turned = (col // 128) % 2 == 1
    low = col % 64 < 32
    lane = col % 64 + jnp.where(turned, jnp.where(low, 32, -32), 0)
    sign = jnp.where(turned & low, -1.0, 1.0)
    spread = jnp.where(row == col // 256 * 64 + lane, sign, 0.0).astype(BF)

    def put(places, x):
        wide = lax.dot_general(
            x.reshape(len(places) * rank, 128),
            spread,
            (((1,), (0,)), ((), ())),
            preferred_element_type=F32,
        ).astype(BF)
        for e, place in enumerate(places):
            for side in range(2):
                for turn in range(2):
                    first = 256 * side + 128 * turn
                    window[place + side, rank * turn : rank * (turn + 1), :] = wide[
                        e * rank : (e + 1) * rank, first : first + 128
                    ]

    @pl.when(pl.program_id(0) == 0)
    def _():
        after = HW + G * chunks * lows
        odd = t[0] % 2
        put([after * (1 - odd) + 2 * e for e in range(HW // 2)], one_ref[...])
        put([after * odd + 2 * e for e in range(HW // 2)], two_ref[...])
        for r in range(chunks):
            for b in range(G):
                group = t[0] ^ (r * G + b)
                put([HW + group * lows + 2 * m for m in range(half)], v_refs[r][b])

    base = pl.program_id(0) * count
    last = None
    for n in range(count):
        parts = [window[base + n + lists[base + n, k]] for k in range(near_count)]
        stacked = jnp.concatenate(parts, axis=0)
        res = lax.dot_general(
            mats_ref[n], stacked, (((1,), (0,)), ((), ())), preferred_element_type=F32
        )
        if n % 2 == 0:
            last = res
        else:
            out_ref[n // 2] = jnp.where(lane_of(res) < 64, last, res)


def near_field(tgt_index, lists, mats, chunks, one, two, G, lows):
    blocks, rank, cols = mats.shape
    near_count = lists.shape[1]
    count = 32
    v_shape = chunks[0].shape

    def spec(shape):
        zeros = (0,) * len(shape)
        return pl.BlockSpec(shape, lambda i, t, o: zeros)

    return pl.pallas_call(
        functools.partial(near_kernel, G, lows, len(chunks), count, near_count),
        out_shape=jax.ShapeDtypeStruct((blocks // 2, rank, 128), F32),
        grid_spec=pltpu.PrefetchScalarGridSpec(
            num_scalar_prefetch=2,
            grid=(blocks // count,),
            in_specs=[spec(v_shape) for _ in chunks]
            + [spec(one.shape), spec(two.shape)]
            + [pl.BlockSpec((count, rank, cols), lambda i, t, o: (i, 0, 0))],
            out_specs=pl.BlockSpec((count // 2, rank, 128), lambda i, t, o: (i, 0, 0)),
            scratch_shapes=[pltpu.VMEM((blocks + 2 * HW, 2 * rank, 128), BF)],
        ),
        compiler_params=params(),
        cost_estimate=cost(6.0),
    )(tgt_index, lists, *chunks, one, two, mats)


def swapped_with(x, axis, distance):
    count = lax.axis_size(axis)
    return lax.ppermute(x, axis, [(i, i ^ distance) for i in range(count)])


def per_device(incident, factors, near_blocks, near_lists):
    groups = lax.axis_size("tgt")
    src_bits = lax.axis_size("src").bit_length() - 1
    tgt_bits = groups.bit_length() - 1
    blocks = incident.shape[1]
    rank = near_blocks.shape[2]
    lows = blocks // groups
    half = lows // 2
    low_bits = lows.bit_length() - 1
    G = 2
    chunks = groups // G
    order = list(range(chunks))[::-1]
    tgt_index = lax.axis_index("tgt").astype(jnp.int32).reshape(1)
    weights = factors[:, 0]
    ends = {0: factors[:1, 0], factors.shape[0] - 1: factors[-1:, 0]}

    def level_weights(level):
        return (ends[level], 0) if level in ends else (weights, level)

    chunk_shape = (G, half, rank, 128)
    chunk_out = jax.ShapeDtypeStruct(chunk_shape, BF)

    def chunk_rows(r, width):
        return pl.BlockSpec((G * lows, width), lambda i, t: ((t[0] // G) ^ r, 0))

    def wspec(level, r):
        return chunk_weights(weights, level, r, G, lows)

    def level_call(level, r, own, other, flip=0):
        array, level = level_weights(level)
        return call(
            functools.partial(level_kernel, G, lows, flip),
            tgt_index,
            (own, other, array),
            [full(chunk_shape), full(chunk_shape), wspec(level, r)],
            chunk_out,
            full(chunk_shape),
            [],
            0.4,
        )

    one, two = edge_pairs(tgt_index, incident[0], rank)
    beside = [(i, i + 1) for i in range(1, groups - 1, 2)]
    one = swapped_with(one, "tgt", 1)
    two = lax.ppermute(two, "tgt", beside + [(j, i) for i, j in beside])
    width = incident.shape[2]
    v = [None] * chunks
    for r in order:
        v[r] = call(
            functools.partial(convert_kernel, G, lows),
            tgt_index,
            (incident[0],),
            [chunk_rows(r, width)],
            chunk_out,
            full(chunk_shape),
            [
                pltpu.VMEM((rank // 2, G * lows, 128), F32),
                pltpu.VMEM((G * half * rank, 128), F32),
            ],
            CONV_US,
        )
    start = list(v)

    level = 0
    for bit in range(src_bits - 1):
        others = [swapped_with(v[r], "src", 1 << bit) for r in order]
        for r, other in zip(order, others):
            v[r] = level_call(level, r, v[r], other)
        level += 1
    arrived = [None] * groups
    for r in order:
        partner = swapped_with(v[r], "src", 1 << (src_bits - 1))
        mixed = call(
            functools.partial(split_kernel, G, lows, low_bits),
            tgt_index,
            (v[r], partner) + (weights,) * (1 + low_bits),
            [full(chunk_shape), full(chunk_shape)]
            + [wspec(level + k, r) for k in range(1 + low_bits)],
            chunk_out,
            full(chunk_shape),
            [],
            1.5,
        )
        moved = swapped_with(mixed, "tgt", r * G) if r else mixed
        for b in range(G):
            arrived[r * G + b] = swapped_with(moved, "tgt", b) if b else moved
    level += 1 + low_bits

    v = call(
        functools.partial(group_kernel, G, lows, groups),
        tgt_index,
        tuple(arrived) + (weights,) * tgt_bits,
        [
            pl.BlockSpec((None,) + chunk_shape[1:], functools.partial(lambda b, i, t: (b, 0, 0, 0), g % G))
            for g in range(groups)
        ]
        + [
            pl.BlockSpec(
                (None, blocks, rank, 128), functools.partial(lambda l, i, t: (l, 0, 0, 0), level + k)
            )
            for k in range(tgt_bits)
        ],
        [chunk_out] * chunks,
        [full(chunk_shape)] * chunks,
        [],
        2.5,
    )
    v = list(v)
    level += tgt_bits
    for bit in range(tgt_bits - 1):
        distance = 1 << bit
        others = [swapped_with(v[r ^ (distance // G)], "tgt", distance) for r in range(chunks)]
        if bit == tgt_bits - 2:
            others[-1], one, two = lax.optimization_barrier((others[-1], one, two))
        v = [level_call(level, r, v[r], others[r], distance % G) for r in range(chunks)]
        level += 1
    near = near_field(tgt_index, near_lists[0], near_blocks[0], start, one, two, G, lows)

    out = None
    distance = 1 << (tgt_bits - 1)
    others = [swapped_with(v[r ^ (distance // G)], "tgt", distance) for r in range(chunks)]
    for r in range(chunks):
        partner = others[r]
        arrays = (v[r], partner, level_weights(level)[0], near)
        specs = [
            full(chunk_shape),
            full(chunk_shape),
            wspec(level_weights(level)[1], r),
            pl.BlockSpec(
                (G * half, rank, 128), functools.partial(lambda r, i, t: ((t[0] // G) ^ r, 0, 0), r)
            ),
        ]
        aliases = None
        if out is not None:
            arrays += (out,)
            specs += [pl.BlockSpec(memory_space=pl.ANY)]
            aliases = {5: 0}
        out = call(
            functools.partial(final_kernel, G, lows, distance % G),
            tgt_index,
            arrays,
            specs,
            jax.ShapeDtypeStruct((blocks, width), F32),
            chunk_rows(r, width),
            [
                pltpu.VMEM((G * half * rank, 128), F32),
                pltpu.VMEM((rank // 2, G * lows, 128), F32),
            ],
            1.2,
            aliases,
        )
    return out[None]


def solution(mesh):
    return jax.shard_map(
        per_device,
        mesh=mesh,
        in_specs=(
            P("src", "tgt", None),
            P(None, "src", "tgt", None, None),
            P("src", "tgt", None, None),
            P("src", "tgt", None),
        ),
        out_specs=P("src", "tgt", None),
        check_vma=False,
    )
```

```python
import functools

import jax
import jax.numpy as jnp
from jax import lax
from jax.experimental import pallas as pl
from jax.experimental.pallas import tpu as pltpu
from jax.sharding import PartitionSpec as P

HW = 4
BF = jnp.bfloat16
F32 = jnp.float32
CONV_US = 2.5
VMEM_LIMIT = 16 * 1024 * 1024


def lane_of(x):
    return lax.broadcasted_iota(jnp.int32, x.shape, 1)


def half_swap(x):
    return pltpu.roll(x, x.shape[1] // 2, 1)


def times_i(x):
    width = x.shape[1]
    quarter = width // 4
    low = pltpu.roll(x, quarter, 1)
    high = pltpu.roll(x, width - quarter, 1)
    return jnp.where(lane_of(x) % (2 * quarter) < quarter, -high, low)


def pick_diag(res):
    rows = res.shape[0] // 2
    top, bottom = res[:rows], res[rows:]
    return jnp.where(lane_of(top) < res.shape[1] // 2, top, bottom)


def with_turn(x):
    return x, times_i(x)


def mix(own, own_i, other, other_i, weights):
    stacked = jnp.concatenate([own, other, own_i, other_i], axis=0)
    res = lax.dot_general(
        weights, stacked, (((1,), (0,)), ((), ())), preferred_element_type=F32
    )
    return pick_diag(res)


def take_weights(w_ref, group, m, lows):
    w = w_ref[pl.ds(group * lows + 2 * m, 2)]
    return w.reshape(2 * w.shape[1], w.shape[2])


def params():
    return pltpu.CompilerParams(vmem_limit_bytes=VMEM_LIMIT)


def cost(us):
    return pl.CostEstimate(flops=0, bytes_accessed=int(us * 3.6e6), transcendentals=0)


def full(shape):
    zeros = (0,) * len(shape)
    return pl.BlockSpec(shape, lambda i, t: zeros)


def chunk_weights(weights, level, r, groups_in, lows):
    _, _, rows, cols = weights.shape
    return pl.BlockSpec(
        (None, groups_in * lows, rows, cols), lambda i, t: (level, (t[0] // groups_in) ^ r, 0, 0)
    )


def call(kernel, tgt_index, arrays, in_specs, out_shapes, out_specs, scratch, us, aliases=None):
    return pl.pallas_call(
        kernel,
        out_shape=out_shapes,
        grid_spec=pltpu.PrefetchScalarGridSpec(
            num_scalar_prefetch=1,
            grid=(1,),
            in_specs=in_specs,
            out_specs=out_specs,
            scratch_shapes=scratch,
        ),
        compiler_params=params(),
        cost_estimate=cost(us),
        input_output_aliases=aliases or {},
    )(tgt_index, *arrays)


def convert_kernel(G, lows, t, inc_ref, out_ref, wide, tall):
    half = lows // 2
    rank = out_ref.shape[2]
    for j in range(rank // 2):
        wide[j] = inc_ref[:, pl.ds(j * 128, 128)].astype(F32)
    for b in range(G):
        group = (t[0] % G) ^ b
        for j in range(rank // 2):
            even = wide[j, pl.ds(group * lows, half, stride=2), :]
            odd = wide[j, pl.ds(group * lows + 1, half, stride=2), :]
            low = lane_of(even) < 64
            tall[pl.ds(b * half * rank + 2 * j, half, stride=rank), :] = jnp.where(
                low, even, half_swap(odd)
            )
            tall[pl.ds(b * half * rank + 2 * j + 1, half, stride=rank), :] = jnp.where(
                low, half_swap(even), odd
            )
    out_ref[...] = tall[...].astype(BF).reshape(out_ref.shape)


def edge_kernel(rows, t, one_ref, two_ref, one_out, two_out, wide, tall):
    pairs, rank, _ = one_out.shape
    even_start = rows - HW
    odd = t[0] % 2
    starts = (even_start * (1 - odd), even_start * odd)
    for ref, out, start in zip((one_ref, two_ref), (one_out, two_out), starts):
        for j in range(rank // 2):
            wide[j] = ref[:, pl.ds(j * 128, 128)].astype(F32)
        for j in range(rank // 2):
            first = wide[j, pl.ds(start, pairs, stride=2), :]
            second = wide[j, pl.ds(start + 1, pairs, stride=2), :]
            low = lane_of(first) < 64
            tall[pl.ds(2 * j, pairs, stride=rank), :] = jnp.where(low, first, half_swap(second))
            tall[pl.ds(2 * j + 1, pairs, stride=rank), :] = jnp.where(
                low, half_swap(first), second
            )
        out[...] = tall[...].astype(BF).reshape(out.shape)


def edge_pairs(tgt_index, incident, rank):
    blocks, width = incident.shape
    rows, pairs = 16, HW // 2
    end = blocks // rows - 1
    shape = jax.ShapeDtypeStruct((pairs, rank, 128), BF)
    return pl.pallas_call(
        functools.partial(edge_kernel, rows),
        out_shape=[shape] * 2,
        grid_spec=pltpu.PrefetchScalarGridSpec(
            num_scalar_prefetch=1,
            grid=(1,),
            in_specs=[
                pl.BlockSpec((rows, width), lambda i, t: (end * (1 - t[0] % 2), 0)),
                pl.BlockSpec((rows, width), lambda i, t: (end * (t[0] % 2), 0)),
            ],
            out_specs=[full(shape.shape)] * 2,
            scratch_shapes=[
                pltpu.VMEM((rank // 2, rows, 128), F32),
                pltpu.VMEM((pairs * rank, 128), F32),
            ],
        ),
        compiler_params=params(),
    )(tgt_index, incident, incident)


def level_kernel(G, lows, flip, t, own_ref, other_ref, w_ref, out_ref):
    half = lows // 2
    for b in range(G):
        group = (t[0] % G) ^ b
        for m in range(half):
            own, own_i = with_turn(own_ref[b, m])
            other, other_i = with_turn(other_ref[b ^ flip, m])
            out_ref[b, m] = mix(
                own, own_i, other, other_i, take_weights(w_ref, group, m, lows)
            ).astype(BF)


def split_kernel(G, lows, low_bits, t, own_ref, other_ref, *rest):
    w_refs = rest[: 1 + low_bits]
    out_ref = rest[1 + low_bits]
    half = lows // 2
    keys = [(b, m) for b in range(G) for m in range(half)]
    groups = [(t[0] % G) ^ b for b in range(G)]
    pairs = {key: with_turn(own_ref[key]) for key in keys}
    others = {key: with_turn(other_ref[key]) for key in keys}
    for bit in range(-1, low_bits):
        if bit == 0:
            others = {key: with_turn(half_swap(pairs[key][0])) for key in keys}
        elif bit > 0:
            others = {(b, m): pairs[b, m ^ (1 << (bit - 1))] for b, m in keys}
        values = {
            (b, m): mix(
                *pairs[b, m],
                *others[b, m],
                take_weights(w_refs[1 + bit], groups[b], m, lows),
            ).astype(BF)
            for b, m in keys
        }
        pairs = {key: with_turn(x) for key, x in values.items()} if bit < low_bits - 1 else values
    for b, m in keys:
        out_ref[b, m] = pairs[b, m]


def group_kernel(G, lows, groups, t, *refs):
    bits = groups.bit_length() - 1
    ins = refs[:groups]
    w_refs = refs[groups : groups + bits]
    outs = refs[groups + bits : groups + bits + groups // G]
    half = lows // 2

    width = max(1, min(half, 64 // groups))
    keys = [(k, g) for k in range(width) for g in range(groups)]

    def body(step, carry):
        values = None
        pairs = {(k, g): with_turn(ins[g][step * width + k]) for k, g in keys}
        for bit in range(bits):
            values = {
                (k, g): mix(
                    *pairs[k, g],
                    *pairs[k, g ^ (1 << bit)],
                    take_weights(w_refs[bit], t[0] ^ g, step * width + k, lows),
                )
                for k, g in keys
            }
            if bit < bits - 1:
                pairs = {key: with_turn(x.astype(BF)) for key, x in values.items()}
        for k, g in keys:
            outs[g // G][g % G, step * width + k] = values[k, g].astype(BF)
        return carry

    lax.fori_loop(0, half // width, body, 0)


def final_kernel(G, lows, flip, t, own_ref, other_ref, w_ref, near_ref, *rest):
    out_ref, tall, wide = rest[-3:]
    half = lows // 2
    rank = own_ref.shape[2]
    for b in range(G):
        group = (t[0] % G) ^ b
        for m in range(half):
            own, own_i = with_turn(own_ref[b, m])
            other, other_i = with_turn(other_ref[b ^ flip, m])
            tall[pl.ds((b * half + m) * rank, rank), :] = (
                mix(own, own_i, other, other_i, take_weights(w_ref, group, m, lows))
                + near_ref[group * half + m]
            )
    for b in range(G):
        group = (t[0] % G) ^ b
        for j in range(rank // 2):
            first = tall[pl.ds(b * half * rank + 2 * j, half, stride=rank), :]
            second = tall[pl.ds(b * half * rank + 2 * j + 1, half, stride=rank), :]
            low = lane_of(first) < 64
            wide[j, pl.ds(group * lows, half, stride=2), :] = jnp.where(
                low, first, half_swap(second)
            )
            wide[j, pl.ds(group * lows + 1, half, stride=2), :] = jnp.where(
                low, half_swap(first), second
            )
    for j in range(rank // 2):
        out_ref[:, pl.ds(j * 128, 128)] = wide[j]


def near_kernel(G, lows, chunks, count, near_count, t, lists, *refs):
    v_refs = refs[:chunks]
    one_ref, two_ref, mats_ref, out_ref, window = refs[chunks : chunks + 5]
    half = lows // 2
    rank = v_refs[0].shape[2]

    row = lax.broadcasted_iota(jnp.int32, (128, 512), 0)
    col = lax.broadcasted_iota(jnp.int32, (128, 512), 1)
    turned = (col // 128) % 2 == 1
    low = col % 64 < 32
    lane = col % 64 + jnp.where(turned, jnp.where(low, 32, -32), 0)
    sign = jnp.where(turned & low, -1.0, 1.0)
    spread = jnp.where(row == col // 256 * 64 + lane, sign, 0.0).astype(BF)

    def put(places, x):
        wide = lax.dot_general(
            x.reshape(len(places) * rank, 128),
            spread,
            (((1,), (0,)), ((), ())),
            preferred_element_type=F32,
        ).astype(BF)
        for e, place in enumerate(places):
            for side in range(2):
                for turn in range(2):
                    first = 256 * side + 128 * turn
                    window[place + side, rank * turn : rank * (turn + 1), :] = wide[
                        e * rank : (e + 1) * rank, first : first + 128
                    ]

    @pl.when(pl.program_id(0) == 0)
    def _():
        after = HW + G * chunks * lows
        odd = t[0] % 2
        put([after * (1 - odd) + 2 * e for e in range(HW // 2)], one_ref[...])
        put([after * odd + 2 * e for e in range(HW // 2)], two_ref[...])
        for r in range(chunks):
            for b in range(G):
                group = t[0] ^ (r * G + b)
                put([HW + group * lows + 2 * m for m in range(half)], v_refs[r][b])

    base = pl.program_id(0) * count
    last = None
    for n in range(count):
        parts = [window[base + n + lists[base + n, k]] for k in range(near_count)]
        stacked = jnp.concatenate(parts, axis=0)
        res = lax.dot_general(
            mats_ref[n], stacked, (((1,), (0,)), ((), ())), preferred_element_type=F32
        )
        if n % 2 == 0:
            last = res
        else:
            out_ref[n // 2] = jnp.where(lane_of(res) < 64, last, res)


def near_field(tgt_index, lists, mats, chunks, one, two, G, lows):
    blocks, rank, cols = mats.shape
    near_count = lists.shape[1]
    count = 32
    v_shape = chunks[0].shape

    def spec(shape):
        zeros = (0,) * len(shape)
        return pl.BlockSpec(shape, lambda i, t, o: zeros)

    return pl.pallas_call(
        functools.partial(near_kernel, G, lows, len(chunks), count, near_count),
        out_shape=jax.ShapeDtypeStruct((blocks // 2, rank, 128), F32),
        grid_spec=pltpu.PrefetchScalarGridSpec(
            num_scalar_prefetch=2,
            grid=(blocks // count,),
            in_specs=[spec(v_shape) for _ in chunks]
            + [spec(one.shape), spec(two.shape)]
            + [pl.BlockSpec((count, rank, cols), lambda i, t, o: (i, 0, 0))],
            out_specs=pl.BlockSpec((count // 2, rank, 128), lambda i, t, o: (i, 0, 0)),
            scratch_shapes=[pltpu.VMEM((blocks + 2 * HW, 2 * rank, 128), BF)],
        ),
        compiler_params=params(),
        cost_estimate=cost(6.0),
    )(tgt_index, lists, *chunks, one, two, mats)


def swapped_with(x, axis, distance):
    count = lax.axis_size(axis)
    return lax.ppermute(x, axis, [(i, i ^ distance) for i in range(count)])


def per_device(incident, factors, near_blocks, near_lists):
    groups = lax.axis_size("tgt")
    src_bits = lax.axis_size("src").bit_length() - 1
    tgt_bits = groups.bit_length() - 1
    blocks = incident.shape[1]
    rank = near_blocks.shape[2]
    lows = blocks // groups
    half = lows // 2
    low_bits = lows.bit_length() - 1
    G = 2
    chunks = groups // G
    order = list(range(chunks))[::-1]
    tgt_index = lax.axis_index("tgt").astype(jnp.int32).reshape(1)
    weights = factors[:, 0]
    ends = {0: factors[:1, 0], factors.shape[0] - 1: factors[-1:, 0]}

    def level_weights(level):
        return (ends[level], 0) if level in ends else (weights, level)

    chunk_shape = (G, half, rank, 128)
    chunk_out = jax.ShapeDtypeStruct(chunk_shape, BF)

    def chunk_rows(r, width):
        return pl.BlockSpec((G * lows, width), lambda i, t: ((t[0] // G) ^ r, 0))

    def wspec(level, r):
        return chunk_weights(weights, level, r, G, lows)

    def level_call(level, r, own, other, flip=0):
        array, level = level_weights(level)
        return call(
            functools.partial(level_kernel, G, lows, flip),
            tgt_index,
            (own, other, array),
            [full(chunk_shape), full(chunk_shape), wspec(level, r)],
            chunk_out,
            full(chunk_shape),
            [],
            0.4,
        )

    one, two = edge_pairs(tgt_index, incident[0], rank)
    beside = [(i, i + 1) for i in range(1, groups - 1, 2)]
    one = swapped_with(one, "tgt", 1)
    two = lax.ppermute(two, "tgt", beside + [(j, i) for i, j in beside])
    width = incident.shape[2]
    v = [None] * chunks
    for r in order:
        v[r] = call(
            functools.partial(convert_kernel, G, lows),
            tgt_index,
            (incident[0],),
            [chunk_rows(r, width)],
            chunk_out,
            full(chunk_shape),
            [
                pltpu.VMEM((rank // 2, G * lows, 128), F32),
                pltpu.VMEM((G * half * rank, 128), F32),
            ],
            CONV_US,
        )
    start = list(v)

    level = 0
    for bit in range(src_bits - 1):
        others = [swapped_with(v[r], "src", 1 << bit) for r in order]
        for r, other in zip(order, others):
            v[r] = level_call(level, r, v[r], other)
        level += 1
    arrived = [None] * groups
    for r in order:
        partner = swapped_with(v[r], "src", 1 << (src_bits - 1))
        mixed = call(
            functools.partial(split_kernel, G, lows, low_bits),
            tgt_index,
            (v[r], partner) + (weights,) * (1 + low_bits),
            [full(chunk_shape), full(chunk_shape)]
            + [wspec(level + k, r) for k in range(1 + low_bits)],
            chunk_out,
            full(chunk_shape),
            [],
            1.5,
        )
        moved = swapped_with(mixed, "tgt", r * G) if r else mixed
        for b in range(G):
            arrived[r * G + b] = swapped_with(moved, "tgt", b) if b else moved
    level += 1 + low_bits

    v = call(
        functools.partial(group_kernel, G, lows, groups),
        tgt_index,
        tuple(arrived) + (weights,) * tgt_bits,
        [
            pl.BlockSpec((None,) + chunk_shape[1:], functools.partial(lambda b, i, t: (b, 0, 0, 0), g % G))
            for g in range(groups)
        ]
        + [
            pl.BlockSpec(
                (None, blocks, rank, 128), functools.partial(lambda l, i, t: (l, 0, 0, 0), level + k)
            )
            for k in range(tgt_bits)
        ],
        [chunk_out] * chunks,
        [full(chunk_shape)] * chunks,
        [],
        2.5,
    )
    v = list(v)
    level += tgt_bits
    for bit in range(tgt_bits - 1):
        distance = 1 << bit
        others = [swapped_with(v[r ^ (distance // G)], "tgt", distance) for r in range(chunks)]
        if bit == tgt_bits - 2:
            others[-1], one, two = lax.optimization_barrier((others[-1], one, two))
        v = [level_call(level, r, v[r], others[r], distance % G) for r in range(chunks)]
        level += 1
    near = near_field(tgt_index, near_lists[0], near_blocks[0], start, one, two, G, lows)

    out = None
    distance = 1 << (tgt_bits - 1)
    others = [swapped_with(v[r ^ (distance // G)], "tgt", distance) for r in range(chunks)]
    for r in range(chunks):
        partner = others[r]
        arrays = (v[r], partner, level_weights(level)[0], near)
        specs = [
            full(chunk_shape),
            full(chunk_shape),
            wspec(level_weights(level)[1], r),
            pl.BlockSpec(
                (G * half, rank, 128), functools.partial(lambda r, i, t: ((t[0] // G) ^ r, 0, 0), r)
            ),
        ]
        aliases = None
        if out is not None:
            arrays += (out,)
            specs += [pl.BlockSpec(memory_space=pl.ANY)]
            aliases = {5: 0}
        out = call(
            functools.partial(final_kernel, G, lows, distance % G),
            tgt_index,
            arrays,
            specs,
            jax.ShapeDtypeStruct((blocks, width), F32),
            chunk_rows(r, width),
            [
                pltpu.VMEM((G * half * rank, 128), F32),
                pltpu.VMEM((rank // 2, G * lows, 128), F32),
            ],
            1.2,
            aliases,
        )
    return out[None]


def solution(mesh):
    return jax.shard_map(
        per_device,
        mesh=mesh,
        in_specs=(
            P("src", "tgt", None),
            P(None, "src", "tgt", None, None),
            P("src", "tgt", None, None),
            P("src", "tgt", None),
        ),
        out_specs=P("src", "tgt", None),
        check_vma=False,
    )
```

```python
import functools

import jax
import jax.numpy as jnp
from jax import lax
from jax.experimental import pallas as pl
from jax.experimental.pallas import tpu as pltpu
from jax.sharding import PartitionSpec as P

HW = 4
BF = jnp.bfloat16
F32 = jnp.float32
CONV_US = 2.5
VMEM_LIMIT = 16 * 1024 * 1024


def lane_of(x):
    return lax.broadcasted_iota(jnp.int32, x.shape, 1)


def half_swap(x):
    return pltpu.roll(x, x.shape[1] // 2, 1)


def times_i(x):
    width = x.shape[1]
    quarter = width // 4
    low = pltpu.roll(x, quarter, 1)
    high = pltpu.roll(x, width - quarter, 1)
    return jnp.where(lane_of(x) % (2 * quarter) < quarter, -high, low)


def pick_diag(res):
    rows = res.shape[0] // 2
    top, bottom = res[:rows], res[rows:]
    return jnp.where(lane_of(top) < res.shape[1] // 2, top, bottom)


def with_turn(x):
    return x, times_i(x)


def mix(own, own_i, other, other_i, weights):
    stacked = jnp.concatenate([own, other, own_i, other_i], axis=0)
    res = lax.dot_general(
        weights, stacked, (((1,), (0,)), ((), ())), preferred_element_type=F32
    )
    return pick_diag(res)


def take_weights(w_ref, group, m, lows):
    w = w_ref[pl.ds(group * lows + 2 * m, 2)]
    return w.reshape(2 * w.shape[1], w.shape[2])


def params():
    return pltpu.CompilerParams(vmem_limit_bytes=VMEM_LIMIT)


def cost(us):
    return pl.CostEstimate(flops=0, bytes_accessed=int(us * 3.6e6), transcendentals=0)


def full(shape):
    zeros = (0,) * len(shape)
    return pl.BlockSpec(shape, lambda i, t: zeros)


def chunk_weights(weights, level, r, groups_in, lows):
    _, _, rows, cols = weights.shape
    return pl.BlockSpec(
        (None, groups_in * lows, rows, cols), lambda i, t: (level, (t[0] // groups_in) ^ r, 0, 0)
    )


def call(kernel, tgt_index, arrays, in_specs, out_shapes, out_specs, scratch, us, aliases=None):
    return pl.pallas_call(
        kernel,
        out_shape=out_shapes,
        grid_spec=pltpu.PrefetchScalarGridSpec(
            num_scalar_prefetch=1,
            grid=(1,),
            in_specs=in_specs,
            out_specs=out_specs,
            scratch_shapes=scratch,
        ),
        compiler_params=params(),
        cost_estimate=cost(us),
        input_output_aliases=aliases or {},
    )(tgt_index, *arrays)


def convert_kernel(G, lows, t, inc_ref, out_ref, wide, tall):
    half = lows // 2
    rank = out_ref.shape[2]
    for j in range(rank // 2):
        wide[j] = inc_ref[:, pl.ds(j * 128, 128)].astype(F32)
    for b in range(G):
        group = (t[0] % G) ^ b
        for j in range(rank // 2):
            even = wide[j, pl.ds(group * lows, half, stride=2), :]
            odd = wide[j, pl.ds(group * lows + 1, half, stride=2), :]
            low = lane_of(even) < 64
            tall[pl.ds(b * half * rank + 2 * j, half, stride=rank), :] = jnp.where(
                low, even, half_swap(odd)
            )
            tall[pl.ds(b * half * rank + 2 * j + 1, half, stride=rank), :] = jnp.where(
                low, half_swap(even), odd
            )
    out_ref[...] = tall[...].astype(BF).reshape(out_ref.shape)


def edge_kernel(rows, t, one_ref, two_ref, one_out, two_out, wide, tall):
    pairs, rank, _ = one_out.shape
    even_start = rows - HW
    odd = t[0] % 2
    starts = (even_start * (1 - odd), even_start * odd)
    for ref, out, start in zip((one_ref, two_ref), (one_out, two_out), starts):
        for j in range(rank // 2):
            wide[j] = ref[:, pl.ds(j * 128, 128)].astype(F32)
        for j in range(rank // 2):
            first = wide[j, pl.ds(start, pairs, stride=2), :]
            second = wide[j, pl.ds(start + 1, pairs, stride=2), :]
            low = lane_of(first) < 64
            tall[pl.ds(2 * j, pairs, stride=rank), :] = jnp.where(low, first, half_swap(second))
            tall[pl.ds(2 * j + 1, pairs, stride=rank), :] = jnp.where(
                low, half_swap(first), second
            )
        out[...] = tall[...].astype(BF).reshape(out.shape)


def edge_pairs(tgt_index, incident, rank):
    blocks, width = incident.shape
    rows, pairs = 16, HW // 2
    end = blocks // rows - 1
    shape = jax.ShapeDtypeStruct((pairs, rank, 128), BF)
    return pl.pallas_call(
        functools.partial(edge_kernel, rows),
        out_shape=[shape] * 2,
        grid_spec=pltpu.PrefetchScalarGridSpec(
            num_scalar_prefetch=1,
            grid=(1,),
            in_specs=[
                pl.BlockSpec((rows, width), lambda i, t: (end * (1 - t[0] % 2), 0)),
                pl.BlockSpec((rows, width), lambda i, t: (end * (t[0] % 2), 0)),
            ],
            out_specs=[full(shape.shape)] * 2,
            scratch_shapes=[
                pltpu.VMEM((rank // 2, rows, 128), F32),
                pltpu.VMEM((pairs * rank, 128), F32),
            ],
        ),
        compiler_params=params(),
    )(tgt_index, incident, incident)


def level_kernel(G, lows, flip, t, own_ref, other_ref, w_ref, out_ref):
    half = lows // 2
    for b in range(G):
        group = (t[0] % G) ^ b
        for m in range(half):
            own, own_i = with_turn(own_ref[b, m])
            other, other_i = with_turn(other_ref[b ^ flip, m])
            out_ref[b, m] = mix(
                own, own_i, other, other_i, take_weights(w_ref, group, m, lows)
            ).astype(BF)


def split_kernel(G, lows, low_bits, t, own_ref, other_ref, *rest):
    w_refs = rest[: 1 + low_bits]
    out_ref = rest[1 + low_bits]
    half = lows // 2
    keys = [(b, m) for b in range(G) for m in range(half)]
    groups = [(t[0] % G) ^ b for b in range(G)]
    pairs = {key: with_turn(own_ref[key]) for key in keys}
    others = {key: with_turn(other_ref[key]) for key in keys}
    for bit in range(-1, low_bits):
        if bit == 0:
            others = {key: with_turn(half_swap(pairs[key][0])) for key in keys}
        elif bit > 0:
            others = {(b, m): pairs[b, m ^ (1 << (bit - 1))] for b, m in keys}
        values = {
            (b, m): mix(
                *pairs[b, m],
                *others[b, m],
                take_weights(w_refs[1 + bit], groups[b], m, lows),
            ).astype(BF)
            for b, m in keys
        }
        pairs = {key: with_turn(x) for key, x in values.items()} if bit < low_bits - 1 else values
    for b, m in keys:
        out_ref[b, m] = pairs[b, m]


def group_kernel(G, lows, groups, t, *refs):
    bits = groups.bit_length() - 1
    ins = refs[:groups]
    w_refs = refs[groups : groups + bits]
    outs = refs[groups + bits : groups + bits + groups // G]
    half = lows // 2

    width = max(1, min(half, 64 // groups))
    keys = [(k, g) for k in range(width) for g in range(groups)]

    def body(step, carry):
        values = None
        pairs = {(k, g): with_turn(ins[g][step * width + k]) for k, g in keys}
        for bit in range(bits):
            values = {
                (k, g): mix(
                    *pairs[k, g],
                    *pairs[k, g ^ (1 << bit)],
                    take_weights(w_refs[bit], t[0] ^ g, step * width + k, lows),
                )
                for k, g in keys
            }
            if bit < bits - 1:
                pairs = {key: with_turn(x.astype(BF)) for key, x in values.items()}
        for k, g in keys:
            outs[g // G][g % G, step * width + k] = values[k, g].astype(BF)
        return carry

    lax.fori_loop(0, half // width, body, 0)


def final_kernel(G, lows, flip, t, own_ref, other_ref, w_ref, near_ref, *rest):
    out_ref, tall, wide = rest[-3:]
    half = lows // 2
    rank = own_ref.shape[2]
    for b in range(G):
        group = (t[0] % G) ^ b
        for m in range(half):
            own, own_i = with_turn(own_ref[b, m])
            other, other_i = with_turn(other_ref[b ^ flip, m])
            tall[pl.ds((b * half + m) * rank, rank), :] = (
                mix(own, own_i, other, other_i, take_weights(w_ref, group, m, lows))
                + near_ref[group * half + m]
            )
    for b in range(G):
        group = (t[0] % G) ^ b
        for j in range(rank // 2):
            first = tall[pl.ds(b * half * rank + 2 * j, half, stride=rank), :]
            second = tall[pl.ds(b * half * rank + 2 * j + 1, half, stride=rank), :]
            low = lane_of(first) < 64
            wide[j, pl.ds(group * lows, half, stride=2), :] = jnp.where(
                low, first, half_swap(second)
            )
            wide[j, pl.ds(group * lows + 1, half, stride=2), :] = jnp.where(
                low, half_swap(first), second
            )
    for j in range(rank // 2):
        out_ref[:, pl.ds(j * 128, 128)] = wide[j]


def near_kernel(G, lows, chunks, count, near_count, t, lists, *refs):
    v_refs = refs[:chunks]
    one_ref, two_ref, mats_ref, out_ref, window = refs[chunks : chunks + 5]
    half = lows // 2
    rank = v_refs[0].shape[2]

    row = lax.broadcasted_iota(jnp.int32, (128, 512), 0)
    col = lax.broadcasted_iota(jnp.int32, (128, 512), 1)
    turned = (col // 128) % 2 == 1
    low = col % 64 < 32
    lane = col % 64 + jnp.where(turned, jnp.where(low, 32, -32), 0)
    sign = jnp.where(turned & low, -1.0, 1.0)
    spread = jnp.where(row == col // 256 * 64 + lane, sign, 0.0).astype(BF)

    def put(places, x):
        wide = lax.dot_general(
            x.reshape(len(places) * rank, 128),
            spread,
            (((1,), (0,)), ((), ())),
            preferred_element_type=F32,
        ).astype(BF)
        for e, place in enumerate(places):
            for side in range(2):
                for turn in range(2):
                    first = 256 * side + 128 * turn
                    window[place + side, rank * turn : rank * (turn + 1), :] = wide[
                        e * rank : (e + 1) * rank, first : first + 128
                    ]

    @pl.when(pl.program_id(0) == 0)
    def _():
        after = HW + G * chunks * lows
        odd = t[0] % 2
        put([after * (1 - odd) + 2 * e for e in range(HW // 2)], one_ref[...])
        put([after * odd + 2 * e for e in range(HW // 2)], two_ref[...])
        for r in range(chunks):
            for b in range(G):
                group = t[0] ^ (r * G + b)
                put([HW + group * lows + 2 * m for m in range(half)], v_refs[r][b])

    base = pl.program_id(0) * count
    last = None
    for n in range(count):
        parts = [window[base + n + lists[base + n, k]] for k in range(near_count)]
        stacked = jnp.concatenate(parts, axis=0)
        res = lax.dot_general(
            mats_ref[n], stacked, (((1,), (0,)), ((), ())), preferred_element_type=F32
        )
        if n % 2 == 0:
            last = res
        else:
            out_ref[n // 2] = jnp.where(lane_of(res) < 64, last, res)


def near_field(tgt_index, lists, mats, chunks, one, two, G, lows):
    blocks, rank, cols = mats.shape
    near_count = lists.shape[1]
    count = 32
    v_shape = chunks[0].shape

    def spec(shape):
        zeros = (0,) * len(shape)
        return pl.BlockSpec(shape, lambda i, t, o: zeros)

    return pl.pallas_call(
        functools.partial(near_kernel, G, lows, len(chunks), count, near_count),
        out_shape=jax.ShapeDtypeStruct((blocks // 2, rank, 128), F32),
        grid_spec=pltpu.PrefetchScalarGridSpec(
            num_scalar_prefetch=2,
            grid=(blocks // count,),
            in_specs=[spec(v_shape) for _ in chunks]
            + [spec(one.shape), spec(two.shape)]
            + [pl.BlockSpec((count, rank, cols), lambda i, t, o: (i, 0, 0))],
            out_specs=pl.BlockSpec((count // 2, rank, 128), lambda i, t, o: (i, 0, 0)),
            scratch_shapes=[pltpu.VMEM((blocks + 2 * HW, 2 * rank, 128), BF)],
        ),
        compiler_params=params(),
        cost_estimate=cost(6.0),
    )(tgt_index, lists, *chunks, one, two, mats)


def swapped_with(x, axis, distance):
    count = lax.axis_size(axis)
    return lax.ppermute(x, axis, [(i, i ^ distance) for i in range(count)])


def per_device(incident, factors, near_blocks, near_lists):
    groups = lax.axis_size("tgt")
    src_bits = lax.axis_size("src").bit_length() - 1
    tgt_bits = groups.bit_length() - 1
    blocks = incident.shape[1]
    rank = near_blocks.shape[2]
    lows = blocks // groups
    half = lows // 2
    low_bits = lows.bit_length() - 1
    G = 2
    chunks = groups // G
    order = list(range(1, chunks)) + [0]
    tgt_index = lax.axis_index("tgt").astype(jnp.int32).reshape(1)
    weights = factors[:, 0]
    ends = {0: factors[:1, 0], factors.shape[0] - 1: factors[-1:, 0]}

    def level_weights(level):
        return (ends[level], 0) if level in ends else (weights, level)

    chunk_shape = (G, half, rank, 128)
    chunk_out = jax.ShapeDtypeStruct(chunk_shape, BF)

    def chunk_rows(r, width):
        return pl.BlockSpec((G * lows, width), lambda i, t: ((t[0] // G) ^ r, 0))

    def wspec(level, r):
        return chunk_weights(weights, level, r, G, lows)

    def level_call(level, r, own, other, flip=0):
        array, level = level_weights(level)
        return call(
            functools.partial(level_kernel, G, lows, flip),
            tgt_index,
            (own, other, array),
            [full(chunk_shape), full(chunk_shape), wspec(level, r)],
            chunk_out,
            full(chunk_shape),
            [],
            0.4,
        )

    one, two = edge_pairs(tgt_index, incident[0], rank)
    beside = [(i, i + 1) for i in range(1, groups - 1, 2)]
    one = swapped_with(one, "tgt", 1)
    two = lax.ppermute(two, "tgt", beside + [(j, i) for i, j in beside])
    width = incident.shape[2]
    v = [None] * chunks
    for r in order:
        v[r] = call(
            functools.partial(convert_kernel, G, lows),
            tgt_index,
            (incident[0],),
            [chunk_rows(r, width)],
            chunk_out,
            full(chunk_shape),
            [
                pltpu.VMEM((rank // 2, G * lows, 128), F32),
                pltpu.VMEM((G * half * rank, 128), F32),
            ],
            CONV_US,
        )
    start = list(v)

    level = 0
    for bit in range(src_bits - 1):
        others = [swapped_with(v[r], "src", 1 << bit) for r in order]
        for r, other in zip(order, others):
            v[r] = level_call(level, r, v[r], other)
        level += 1
    arrived = [None] * groups
    for r in order:
        partner = swapped_with(v[r], "src", 1 << (src_bits - 1))
        mixed = call(
            functools.partial(split_kernel, G, lows, low_bits),
            tgt_index,
            (v[r], partner) + (weights,) * (1 + low_bits),
            [full(chunk_shape), full(chunk_shape)]
            + [wspec(level + k, r) for k in range(1 + low_bits)],
            chunk_out,
            full(chunk_shape),
            [],
            1.5,
        )
        moved = swapped_with(mixed, "tgt", r * G) if r else mixed
        for b in range(G):
            arrived[r * G + b] = swapped_with(moved, "tgt", b) if b else moved
    level += 1 + low_bits

    v = call(
        functools.partial(group_kernel, G, lows, groups),
        tgt_index,
        tuple(arrived) + (weights,) * tgt_bits,
        [
            pl.BlockSpec((None,) + chunk_shape[1:], functools.partial(lambda b, i, t: (b, 0, 0, 0), g % G))
            for g in range(groups)
        ]
        + [
            pl.BlockSpec(
                (None, blocks, rank, 128), functools.partial(lambda l, i, t: (l, 0, 0, 0), level + k)
            )
            for k in range(tgt_bits)
        ],
        [chunk_out] * chunks,
        [full(chunk_shape)] * chunks,
        [],
        2.5,
    )
    v = list(v)
    level += tgt_bits
    for bit in range(tgt_bits - 1):
        distance = 1 << bit
        others = [swapped_with(v[r ^ (distance // G)], "tgt", distance) for r in range(chunks)]
        if bit == tgt_bits - 2:
            others[-1], one, two = lax.optimization_barrier((others[-1], one, two))
        v = [level_call(level, r, v[r], others[r], distance % G) for r in range(chunks)]
        level += 1
    near = near_field(tgt_index, near_lists[0], near_blocks[0], start, one, two, G, lows)

    out = None
    distance = 1 << (tgt_bits - 1)
    others = [swapped_with(v[r ^ (distance // G)], "tgt", distance) for r in range(chunks)]
    for r in range(chunks):
        partner = others[r]
        arrays = (v[r], partner, level_weights(level)[0], near)
        specs = [
            full(chunk_shape),
            full(chunk_shape),
            wspec(level_weights(level)[1], r),
            pl.BlockSpec(
                (G * half, rank, 128), functools.partial(lambda r, i, t: ((t[0] // G) ^ r, 0, 0), r)
            ),
        ]
        aliases = None
        if out is not None:
            arrays += (out,)
            specs += [pl.BlockSpec(memory_space=pl.ANY)]
            aliases = {5: 0}
        out = call(
            functools.partial(final_kernel, G, lows, distance % G),
            tgt_index,
            arrays,
            specs,
            jax.ShapeDtypeStruct((blocks, width), F32),
            chunk_rows(r, width),
            [
                pltpu.VMEM((G * half * rank, 128), F32),
                pltpu.VMEM((rank // 2, G * lows, 128), F32),
            ],
            1.2,
            aliases,
        )
    return out[None]


def solution(mesh):
    return jax.shard_map(
        per_device,
        mesh=mesh,
        in_specs=(
            P("src", "tgt", None),
            P(None, "src", "tgt", None, None),
            P("src", "tgt", None, None),
            P("src", "tgt", None),
        ),
        out_specs=P("src", "tgt", None),
        check_vma=False,
    )
```
